512 devices in a mesh: tm: 16 (over y, z_lo), space: 32 (over z_hi, x, core).
Axes of the slice: x: 4, y: 8, z: 8 (z_hi: 4, z_lo: 2; z = z_hi * 2 + z_lo), core: 2. Of those that a mesh axis runs over, the one named last changes fastest.
Arguments:
- initial: float32 [2048, 128], P('space'), may hold values from -6 to 6
- block_inverse: float32 [128, 128], replicated, may hold values from -0.2 to 0.95
- coupling: bfloat16 [6, 3, 128, 128], replicated, may hold values from -0.078125 to 0.078125
- neighbours: int32 [2048, 6], P('space'), may hold values from -1 to 127, as said below
- orientation: int32 [2048, 6], P('space'), may hold values from 0 to 2
- step_counts: int32 [16], P('tm'), may hold values from 1 to 4, as said below
Outputs:
- slice_ends: float32 [16, 2048, 128], P('tm', 'space')
The draws below stay inside these ranges and needn't reach their ends.
Inputs may be any that keep to these rules, and one draw needn't show every extreme that they name: `neighbours`: entry f (faces -x, +x, -y, +y, -z, +z) of an element is -1 for a closed face, else the row of the element across that face in this device's block of 64 rows preceded by the 32 last rows of the device below and followed by the 32 first rows of the device above; a device's elements form a grid of 4 x 8 x 2 numbered first dimension fastest, and a face is open from both sides or from neither. `step_counts`: some slice takes 4 steps.
All inputs are finite; a program needn't handle non-finite values.
Results may differ from the reference program's by a relative error of at most 0.0029.
Values may be sent and summed in bfloat16 or wider, within the bound.
A program may use at most 64 MiB of HBM per device.

```python
import jax
import jax.numpy as jnp
from jax import lax

NP = 128
NORI = 3
FSTEPS = 4
SWEEPS = 3
ITERS = 2
EX = 4
EY = 8
FL = 32
E_DEV = 64
NE = 2048
TSL = 16


def draw_block_inverse(key, part):
    key = jax.random.fold_in(key, 11)
    random_part = jax.random.normal(key, (NP, NP), jnp.float32)
    skew_part = (random_part - random_part.T) * (0.017 / 1.41421356)
    return 0.95 * jnp.eye(NP, dtype=jnp.float32) + skew_part


def draw_neighbours(key, part):
    key = jax.random.fold_in(key, 12)
    key_x, key_y, key_z = jax.random.split(key, 3)
    rows = jnp.arange(NE, dtype=jnp.int32)
    local_row = rows % E_DEV
    place_x = local_row % EX
    place_y = local_row // EX % EY
    open_x = jax.random.randint(key_x, (NE,), 0, 5) != 0
    open_y = jax.random.randint(key_y, (NE,), 0, 5) != 0
    open_z = jax.random.randint(key_z, (NE,), 0, 5) != 0
    closed = jnp.full((NE,), -1, jnp.int32)
    minus_x = jnp.where((place_x > 0) & jnp.roll(open_x, 1), local_row + FL - 1, closed)
    plus_x = jnp.where((place_x < EX - 1) & open_x, local_row + FL + 1, closed)
    minus_y = jnp.where((place_y > 0) & jnp.roll(open_y, EX), local_row + FL - EX, closed)
    plus_y = jnp.where((place_y < EY - 1) & open_y, local_row + FL + EX, closed)
    minus_z = jnp.where((rows >= FL) & jnp.roll(open_z, FL), local_row, closed)
    plus_z = jnp.where((rows < NE - FL) & open_z, local_row + 2 * FL, closed)
    return jnp.stack([minus_x, plus_x, minus_y, plus_y, minus_z, plus_z], axis=1).astype(jnp.int32)


def draw_step_counts(key, part):
    key = jax.random.fold_in(key, 13)
    key_counts, key_spot = jax.random.split(key)
    counts = jax.random.randint(key_counts, (TSL,), 1, FSTEPS + 1)
    spot = jax.random.randint(key_spot, (), 0, TSL)
    return counts.at[spot].set(FSTEPS).astype(jnp.int32)


def with_ends(array, own_key, least, high):
    longest = array.shape.index(max(array.shape))
    spots = []
    for shift in (0, 1):
        where = [jax.random.randint(jax.random.fold_in(own_key, axis), (), 0, length) for axis, length in enumerate(array.shape)]
        where[longest] = (where[longest] + shift) % array.shape[longest]
        spots.append(tuple(where))
    return array.at[spots[0]].set(least).at[spots[1]].set(high)


def level_of(stream_key, shape, cuts, low, largest):
    level, own = 1.0, jax.random.fold_in(stream_key, 6)
    for dim, shards_of in cuts:
        heights = jnp.exp(jax.random.uniform(jax.random.fold_in(own, dim), (shards_of,), jnp.float32, low / len(cuts), largest / len(cuts)))
        level = level * jnp.repeat(heights, shape[dim] // shards_of).reshape([-1 if axis == dim else 1 for axis in range(len(shape))])
    return level


def bell_draw(own_key, extent, scale, bound, cuts=(), kind=jnp.bfloat16):
    entries = jax.random.normal(own_key, extent, jnp.float32) * scale
    if len(cuts) > 0:
        entries = level_of(own_key, extent, cuts, -0.22, 0.18) * entries
    return jnp.clip(entries, min=-bound, max=bound).astype(kind)


def setup_inputs(seed: int = 0) -> dict:
    key_of = jax.random.split(jax.random.key(seed), 7)
    initial = bell_draw(key_of[0], (NE, NP), 1.0, 6.0, ((0, 32),), jnp.float32)
    block_inverse = draw_block_inverse(jax.random.fold_in(key_of[6], 71), 0)
    coupling = bell_draw(key_of[2], (6, NORI, NP, NP), (NP * 40) ** -0.5, 0.078125)
    neighbours = draw_neighbours(jax.random.fold_in(key_of[6], 71), 0)
    orientation = with_ends(jax.random.randint(key_of[4], (NE, 6), 0, NORI), jax.random.fold_in(key_of[4], 1), 0, NORI - 1).astype(jnp.int32)
    step_counts = draw_step_counts(jax.random.fold_in(key_of[6], 71), 0)
    return {"initial": initial, "block_inverse": block_inverse, "coupling": coupling, "neighbours": neighbours, "orientation": orientation, "step_counts": step_counts}


def apply_block(values, matrix):
    return jnp.dot(values, matrix, precision=lax.Precision.HIGHEST)


def couple(rounded, gather_rows, usable, orientation, coupling):
    summed = jnp.zeros(rounded.shape, jnp.float32)
    nothing = jnp.zeros((), jnp.bfloat16)
    for face_no in range(6):
        picked = jnp.where(usable[None, :, face_no, None], rounded[:, gather_rows[:, face_no], :], nothing)
        for orient_no in range(NORI):
            masked = jnp.where((orientation[:, face_no] == orient_no)[None, :, None], picked, nothing)
            product = jnp.dot(masked.reshape(-1, NP), coupling[face_no, orient_no], preferred_element_type=jnp.float32)
            summed = summed + product.reshape(summed.shape)
    return summed


def reference(initial, block_inverse, coupling, neighbours, orientation, step_counts):
    rows = jnp.arange(NE, dtype=jnp.int32)
    global_row = ((rows // E_DEV) * E_DEV - FL)[:, None] + neighbours
    usable = (neighbours >= 0) & (global_row >= 0) & (global_row < NE)
    gather_rows = jnp.clip(global_row, 0, NE - 1).astype(jnp.int32)

    def fine_solve(states):
        current = states
        for step_no in range(FSTEPS):
            iterate = current
            for sweep_no in range(SWEEPS):
                rounded = iterate.astype(jnp.bfloat16)
                iterate = apply_block(current - couple(rounded, gather_rows, usable, orientation, coupling), block_inverse)
            current = jnp.where((step_no < step_counts)[:, None, None], iterate, current)
        return current

    starts = [initial]
    for slice_no in range(TSL - 1):
        starts.append(apply_block(starts[-1], block_inverse))
    starts = jnp.stack(starts)
    finish = starts
    for iter_no in range(ITERS):
        defect = fine_solve(starts) - apply_block(starts, block_inverse)
        fresh = [initial]
        for slice_no in range(TSL - 1):
            fresh.append(apply_block(fresh[-1], block_inverse) + defect[slice_no])
        starts = jnp.stack(fresh)
        finish = apply_block(starts, block_inverse) + defect
    return finish
```

```python
import jax
import jax.numpy as jnp
from jax import lax
from jax.experimental import pallas as pl
from jax.experimental.pallas import tpu as pltpu
from jax.sharding import PartitionSpec as P

NP = 128
NORI = 3
FSTEPS = 4
SWEEPS = 3
ITERS = 2
FL = 32
ROWS = 64
DEPTH = FSTEPS * SWEEPS * FL // ROWS
SPAN = 2 * DEPTH + 1
EXT = SPAN * ROWS
OWN = DEPTH * ROWS
SHIFTS = (-1, 1, -4, 4, -FL, FL)
MESH = pl.DeviceIdType.MESH
BF = jnp.bfloat16
F32 = jnp.float32


def row_blocks(low, high):
    units = (high - low) // 16
    count = -(-units // 12)
    cuts = [low + 16 * (units * i // count) for i in range(count + 1)]
    return [(a, b - a) for a, b in zip(cuts[:-1], cuts[1:])]


def split(values):
    head = values.astype(BF)
    return head, (values - head.astype(F32)).astype(BF)


def exact_dot(values, matrix):
    return jnp.dot(values, matrix, precision=lax.Precision.HIGHEST, preferred_element_type=F32)


def halves(product):
    return product[:, :NP] + product[:, NP:]


def kernel(
    tm_size, space_size,
    initial, inverse, coupling, neighbours, orientation, counts, out,
    powers, stacked, inverse_pair, weights, mask, meta, codes, sent, halo, gone, come,
    current, following, iterate, coarse, state, first,
    meta_send, meta_recv, halo_send, halo_recv, come_send, come_recv,
):
    here = lax.axis_index("space")
    slice_no = lax.axis_index("tm")
    offsets = [d for k in range(DEPTH, 0, -1) for d in (-k, k)]

    def at_space(by):
        return {"space": lax.rem(here + (by + space_size), space_size)}

    def at_tm(by):
        return {"tm": lax.rem(slice_no + (by + tm_size), tm_size)}

    barrier = pltpu.get_barrier_semaphore()
    for d in offsets:
        pl.semaphore_signal(barrier, inc=1, device_id=at_space(d), device_id_type=MESH)
    for j in range(1, tm_size):
        pl.semaphore_signal(barrier, inc=1, device_id=at_tm(j), device_id_type=MESH)

    def meta_copy(d):
        return pltpu.make_async_remote_copy(
            src_ref=meta, dst_ref=codes.at[DEPTH - d],
            send_sem=meta_send.at[DEPTH - d], recv_sem=meta_recv.at[DEPTH - d],
            device_id=at_space(d), device_id_type=MESH,
        )

    def halo_copy(it, d):
        return pltpu.make_async_remote_copy(
            src_ref=sent.at[it], dst_ref=halo.at[it, DEPTH - d],
            send_sem=halo_send.at[it, DEPTH - d], recv_sem=halo_recv.at[it, DEPTH - d],
            device_id=at_space(d), device_id_type=MESH,
        )

    def defect_copy(it, j):
        return pltpu.make_async_remote_copy(
            src_ref=gone.at[it], dst_ref=come.at[it, j - 1],
            send_sem=come_send.at[it, j - 1], recv_sem=come_recv.at[it, j - 1],
            device_id=at_tm(j), device_id_type=MESH,
        )

    found = neighbours[...]
    place = found + here * ROWS
    usable = (found >= 0) & (place >= FL) & (place < space_size * ROWS + FL)
    meta[...] = jnp.zeros_like(meta)
    meta[:6, :ROWS] = jnp.where(usable, orientation[...], NORI).astype(F32)
    codes[DEPTH] = meta[...]
    codes[SPAN:] = jnp.zeros((16 - SPAN, 8, NP), F32)
    for j in range(1, tm_size):
        @pl.when(slice_no < j)
        def _():
            come[:, j - 1] = jnp.zeros((ITERS, ROWS, NP), BF)

    rows = lax.broadcasted_iota(jnp.int32, (NP, NP), 0)
    columns = lax.broadcasted_iota(jnp.int32, (NP, NP), 1)
    powers[:NP] = (rows == columns).astype(F32)
    powers[NP : 2 * NP] = inverse[...]
    known = 1
    while known < tm_size - 1:
        more = min(known, tm_size - 1 - known)
        last = powers[known * NP : (known + 1) * NP]
        powers[(known + 1) * NP : (known + 1 + more) * NP] = exact_dot(
            powers[NP : (1 + more) * NP], last
        )
        known += more
    mine = powers[pl.ds(pl.multiple_of(slice_no * NP, NP), NP)]
    first[...] = exact_dot(initial[...], mine)
    state[...] = first[...]
    sent[0] = first[...].astype(BF)

    pl.semaphore_wait(barrier, len(offsets) + tm_size - 1)
    for d in offsets:
        meta_copy(d).start()
    for d in offsets:
        halo_copy(0, d).start()

    head, tail = split(inverse[...])
    inverse_pair[:NP, :NP] = head
    inverse_pair[NP:, :NP] = head
    inverse_pair[:NP, NP:] = tail
    inverse_pair[NP:, NP:] = jnp.zeros_like(tail)
    for j in range(2, tm_size):
        lines = pl.ds((j - 2) * NP, NP)
        head, tail = split(powers[(j - 1) * NP : j * NP])
        stacked[lines, :NP] = head
        stacked[lines, NP:] = tail
    for part in range(6 * NORI):
        lines = pl.ds(part * NP, NP)
        folded = halves(
            jnp.dot(coupling[lines], inverse_pair[:NP], preferred_element_type=F32)
        )
        head, tail = split(folded)
        weights[lines, :NP] = head
        weights[lines, NP:] = tail

    for d in offsets:
        meta_copy(d).wait_recv()
    turned = jnp.transpose(codes[...].reshape(NP, NP))
    for place_no in range(SPAN):
        for face in range(6):
            column = place_no * 8 + face
            code = jnp.broadcast_to(turned[:ROWS, column : column + 1], (ROWS, NP)).astype(BF)
            for kind in range(NORI):
                mask[face * NORI + kind, place_no * ROWS : (place_no + 1) * ROWS] = jnp.where(
                    code == jnp.array(kind, BF), jnp.array(1, BF), jnp.array(0, BF)
                )

    steps_here = counts[0]

    def iteration(it, _):
        for d in offsets:
            halo_copy(it, d).wait_recv()
        for place_no in range(SPAN):
            lines = pl.ds(place_no * ROWS, ROWS)
            if place_no == DEPTH:
                current[lines] = state[...]
            else:
                current[lines] = halo[it, place_no].astype(F32)
        now, later = current, following
        for step in range(FSTEPS):
            for sweep in range(SWEEPS):
                reach = FL * (step * SWEEPS + sweep + 1)
                source = now if sweep == 0 else iterate.at[sweep - 1]
                for low, height in row_blocks(reach, EXT - reach):
                    lines = pl.ds(low, height)
                    picked = []
                    for face, shift in enumerate(SHIFTS):
                        rounded = source[pl.ds(low + shift, height)].astype(BF)
                        for kind in range(NORI):
                            picked.append(rounded * mask[face * NORI + kind, lines])
                    coupled = halves(
                        jnp.dot(
                            jnp.concatenate(picked, axis=1),
                            weights[...],
                            preferred_element_type=F32,
                        )
                    )
                    if sweep == 0:
                        ahead = halves(
                            jnp.dot(
                                jnp.concatenate(split(now[lines]), axis=1),
                                inverse_pair[...],
                                preferred_element_type=F32,
                            )
                        )
                        coarse[step, lines] = ahead
                    else:
                        ahead = coarse[step, lines]
                    update = ahead - coupled
                    if sweep < SWEEPS - 1:
                        iterate[sweep, lines] = update
                    else:
                        later[lines] = jnp.where(step < steps_here, update, now[lines])
            now, later = later, now
        own = pl.ds(OWN, ROWS)
        defect = now[own] - coarse[0, own]
        out[...] = defect
        gone[it] = defect.astype(BF)
        for j in range(tm_size - 1, 0, -1):
            @pl.when(slice_no + j < tm_size)
            def _():
                defect_copy(it, j).start()
        for j in range(tm_size - 1, 0, -1):
            @pl.when(slice_no >= j)
            def _():
                defect_copy(it, j).wait_recv()
        arrived = jnp.concatenate([come[it, j] for j in range(1, tm_size - 1)], axis=1)
        total = halves(jnp.dot(arrived, stacked[...], preferred_element_type=F32))
        fresh = first[...] + come[it, 0].astype(F32) + total
        state[...] = fresh

        @pl.when(it == 0)
        def _():
            sent[1] = fresh.astype(BF)
            for d in offsets:
                halo_copy(1, d).start()

        return 0

    lax.fori_loop(0, ITERS, iteration, 0)
    out[...] = out[...] + exact_dot(state[...], inverse[...])

    for d in offsets:
        meta_copy(d).wait_send()
        for it in range(ITERS):
            halo_copy(it, d).wait_send()
    for j in range(1, tm_size):
        @pl.when(slice_no + j < tm_size)
        def _():
            for it in range(ITERS):
                defect_copy(it, j).wait_send()


def solution(mesh):
    tm_size, space_size = mesh.shape["tm"], mesh.shape["space"]

    def per_device(initial, inverse, coupling, neighbours, orientation, counts):
        vmem = pl.BlockSpec(memory_space=pltpu.VMEM)
        dma = pltpu.SemaphoreType.DMA

        def body(*refs):
            kernel(tm_size, space_size, *refs)

        finish = pl.pallas_call(
            body,
            out_shape=jax.ShapeDtypeStruct((ROWS, NP), F32),
            in_specs=[vmem] * 5 + [pl.BlockSpec(memory_space=pltpu.SMEM)],
            out_specs=vmem,
            scratch_shapes=[
                pltpu.VMEM((tm_size * NP, NP), F32),
                pltpu.VMEM(((tm_size - 2) * NP, 2 * NP), BF),
                pltpu.VMEM((2 * NP, 2 * NP), BF),
                pltpu.VMEM((6 * NORI * NP, 2 * NP), BF),
                pltpu.VMEM((6 * NORI, EXT, NP), BF),
                pltpu.VMEM((8, NP), F32),
                pltpu.VMEM((16, 8, NP), F32),
                pltpu.VMEM((ITERS, ROWS, NP), BF),
                pltpu.VMEM((ITERS, SPAN, ROWS, NP), BF),
                pltpu.VMEM((ITERS, ROWS, NP), BF),
                pltpu.VMEM((ITERS, tm_size - 1, ROWS, NP), BF),
                pltpu.VMEM((EXT, NP), F32),
                pltpu.VMEM((EXT, NP), F32),
                pltpu.VMEM((SWEEPS - 1, EXT, NP), F32),
                pltpu.VMEM((FSTEPS, EXT, NP), F32),
                pltpu.VMEM((ROWS, NP), F32),
                pltpu.VMEM((ROWS, NP), F32),
                dma((SPAN,)),
                dma((SPAN,)),
                dma((ITERS, SPAN)),
                dma((ITERS, SPAN)),
                dma((ITERS, tm_size - 1)),
                dma((ITERS, tm_size - 1)),
            ],
            compiler_params=pltpu.CompilerParams(
                collective_id=0, has_side_effects=True, vmem_limit_bytes=40 << 20
            ),
            name="parareal",
        )(
            initial,
            inverse,
            coupling.reshape(6 * NORI * NP, NP),
            neighbours.T,
            orientation.T,
            counts,
        )
        return finish[None]

    return jax.shard_map(
        per_device,
        mesh=mesh,
        in_specs=(P("space", None), P(), P(), P("space", None), P("space", None), P("tm")),
        out_specs=P("tm", "space", None),
        check_vma=False,
    )
```

```python
import jax
import jax.numpy as jnp
from jax import lax
from jax.experimental import pallas as pl
from jax.experimental.pallas import tpu as pltpu
from jax.sharding import PartitionSpec as P

NP = 128
NORI = 3
FSTEPS = 4
SWEEPS = 3
ITERS = 2
FL = 32
ROWS = 64
DEPTH = FSTEPS * SWEEPS * FL // ROWS
SPAN = 2 * DEPTH + 1
EXT = SPAN * ROWS
OWN = DEPTH * ROWS
SHIFTS = (-1, 1, -4, 4, -FL, FL)
MESH = pl.DeviceIdType.MESH
BF = jnp.bfloat16
F32 = jnp.float32


def row_blocks(low, high):
    units = (high - low) // 16
    count = -(-units // 24)
    cuts = [low + 16 * (units * i // count) for i in range(count + 1)]
    return [(a, b - a) for a, b in zip(cuts[:-1], cuts[1:])]


def split(values):
    head = values.astype(BF)
    return head, (values - head.astype(F32)).astype(BF)


def exact_dot(values, matrix):
    return jnp.dot(values, matrix, precision=lax.Precision.HIGHEST, preferred_element_type=F32)


def halves(product):
    return product[:, :NP] + product[:, NP:]


def kernel(
    tm_size, space_size,
    initial_hbm, inverse_hbm, coupling_hbm, neighbours_hbm, orientation_hbm, counts_hbm, out,
    initial, inverse, coupling, neighbours, orientation, counts,
    powers, stacked, inverse_pair, weights, mask, meta, codes, sent, halo, gone, come,
    current, following, iterate, coarse, state, first,
    load_done, meta_send, meta_recv, halo_send, halo_recv, come_send, come_recv,
):
    here = lax.axis_index("space")
    slice_no = lax.axis_index("tm")
    offsets = [d for k in range(DEPTH, 0, -1) for d in (-k, k)]
    near = offsets[::-1]

    def at_space(by):
        return {"space": lax.rem(here + (by + space_size), space_size)}

    def at_tm(by):
        return {"tm": lax.rem(slice_no + (by + tm_size), tm_size)}

    def has(by):
        return here + by >= 0 if by < 0 else here + by < space_size

    barrier = pltpu.get_barrier_semaphore()
    for d in offsets:
        @pl.when(has(d))
        def _():
            pl.semaphore_signal(barrier, inc=1, device_id=at_space(d), device_id_type=MESH)
    for j in range(tm_size - 1, 0, -1):
        @pl.when(slice_no >= j)
        def _():
            pl.semaphore_signal(barrier, inc=1, device_id=at_tm(-j), device_id_type=MESH)

    loads = [
        pltpu.make_async_copy(source, target, load_done.at[i])
        for i, (source, target) in enumerate((
            (neighbours_hbm, neighbours),
            (orientation_hbm, orientation),
            (inverse_hbm, inverse),
            (initial_hbm, initial),
            (coupling_hbm, coupling),
            (counts_hbm, counts),
        ))
    ]
    for load in loads:
        load.start()

    def meta_copy(d):
        return pltpu.make_async_remote_copy(
            src_ref=meta, dst_ref=codes.at[DEPTH - d],
            send_sem=meta_send.at[DEPTH - d], recv_sem=meta_recv.at[DEPTH - d],
            device_id=at_space(d), device_id_type=MESH,
        )

    def halo_copy(it, d):
        return pltpu.make_async_remote_copy(
            src_ref=sent.at[it], dst_ref=halo.at[it, DEPTH - d],
            send_sem=halo_send.at[it, DEPTH - d], recv_sem=halo_recv.at[it, DEPTH - d],
            device_id=at_space(d), device_id_type=MESH,
        )

    def defect_copy(it, j):
        return pltpu.make_async_remote_copy(
            src_ref=gone.at[it], dst_ref=come.at[it, j - 1],
            send_sem=come_send.at[it, j - 1], recv_sem=come_recv.at[it, j - 1],
            device_id=at_tm(j), device_id_type=MESH,
        )

    for j in range(1, tm_size):
        @pl.when(slice_no < j)
        def _():
            come[:, j - 1] = jnp.zeros((ITERS, ROWS, NP), BF)
    codes[SPAN:] = jnp.zeros((16 - SPAN, 8, NP), F32)
    for d in offsets:
        @pl.when(jnp.logical_not(has(d)))
        def _():
            codes[DEPTH + d] = jnp.zeros((8, NP), F32)
            halo[:, DEPTH + d] = jnp.zeros((ITERS, ROWS, NP), BF)

    loads[0].wait()
    loads[1].wait()
    found = neighbours[...]
    place = found + here * ROWS
    usable = (found >= 0) & (place >= FL) & (place < space_size * ROWS + FL)
    meta[...] = jnp.zeros_like(meta)
    meta[:6, :ROWS] = jnp.where(usable, orientation[...], NORI).astype(F32)
    codes[DEPTH] = meta[...]

    rows = lax.broadcasted_iota(jnp.int32, (NP, NP), 0)
    columns = lax.broadcasted_iota(jnp.int32, (NP, NP), 1)
    loads[2].wait()
    powers[:NP] = (rows == columns).astype(F32)
    powers[NP : 2 * NP] = inverse[...]
    known = 1
    while known < tm_size - 1:
        more = min(known, tm_size - 1 - known)
        last = powers[known * NP : (known + 1) * NP]
        powers[(known + 1) * NP : (known + 1 + more) * NP] = exact_dot(
            powers[NP : (1 + more) * NP], last
        )
        known += more
    mine = powers[pl.ds(pl.multiple_of(slice_no * NP, NP), NP)]
    loads[3].wait()
    first[...] = exact_dot(initial[...], mine)
    state[...] = first[...]
    sent[0] = first[...].astype(BF)

    peers = (
        jnp.minimum(here, DEPTH) + jnp.minimum(space_size - 1 - here, DEPTH) + tm_size - 1 - slice_no
    )
    pl.semaphore_wait(barrier, peers)
    for d in offsets:
        @pl.when(has(d))
        def _():
            meta_copy(d).start()
            halo_copy(0, d).start()

    head, tail = split(inverse[...])
    inverse_pair[:NP, :NP] = head
    inverse_pair[NP:, :NP] = head
    inverse_pair[:NP, NP:] = tail
    inverse_pair[NP:, NP:] = jnp.zeros_like(tail)
    for j in range(2, tm_size):
        lines = pl.ds((j - 2) * NP, NP)
        head, tail = split(powers[(j - 1) * NP : j * NP])
        stacked[lines, :NP] = head
        stacked[lines, NP:] = tail
    loads[4].wait()
    for part in range(6 * NORI):
        lines = pl.ds(part * NP, NP)
        folded = halves(
            jnp.dot(coupling[lines], inverse_pair[:NP], preferred_element_type=F32)
        )
        head, tail = split(folded)
        weights[lines, :NP] = head
        weights[lines, NP:] = tail

    for d in near:
        @pl.when(has(d))
        def _():
            meta_copy(-d).wait_recv()
    turned = jnp.transpose(codes[...].reshape(NP, NP))
    for place_no in range(SPAN):
        for face in range(6):
            column = place_no * 8 + face
            code = jnp.broadcast_to(turned[:ROWS, column : column + 1], (ROWS, NP)).astype(BF)
            for kind in range(NORI):
                mask[face * NORI + kind, place_no * ROWS : (place_no + 1) * ROWS] = jnp.where(
                    code == jnp.array(kind, BF), jnp.array(1, BF), jnp.array(0, BF)
                )

    loads[5].wait()
    steps_here = counts[0]

    def iteration(it, _):
        for d in near:
            @pl.when(has(d))
            def _():
                halo_copy(it, -d).wait_recv()
        for place_no in range(SPAN):
            lines = pl.ds(place_no * ROWS, ROWS)
            if place_no == DEPTH:
                current[lines] = state[...]
            else:
                current[lines] = halo[it, place_no].astype(F32)
        now, later = current, following
        for step in range(FSTEPS):
            for sweep in range(SWEEPS):
                reach = FL * (step * SWEEPS + sweep + 1)
                source = now if sweep == 0 else iterate.at[sweep - 1]
                for low, height in row_blocks(reach, EXT - reach):
                    lines = pl.ds(low, height)
                    picked = []
                    for face, shift in enumerate(SHIFTS):
                        rounded = source[pl.ds(low + shift, height)].astype(BF)
                        for kind in range(NORI):
                            picked.append(rounded * mask[face * NORI + kind, lines])
                    coupled = sum(
                        halves(
                            jnp.dot(
                                jnp.concatenate(picked[part : part + 2], axis=1),
                                weights[part * NP : (part + 2) * NP],
                                preferred_element_type=F32,
                            )
                        )
                        for part in range(0, 6 * NORI, 2)
                    )
                    if sweep == 0:
                        ahead = halves(
                            jnp.dot(
                                jnp.concatenate(split(now[lines]), axis=1),
                                inverse_pair[...],
                                preferred_element_type=F32,
                            )
                        )
                        coarse[step, lines] = ahead
                    else:
                        ahead = coarse[step, lines]
                    update = ahead - coupled
                    if sweep < SWEEPS - 1:
                        iterate[sweep, lines] = update
                    else:
                        later[lines] = jnp.where(step < steps_here, update, now[lines])
            now, later = later, now
        own = pl.ds(OWN, ROWS)
        defect = now[own] - coarse[0, own]
        out[...] = defect
        gone[it] = defect.astype(BF)
        for j in range(tm_size - 1, 0, -1):
            @pl.when(slice_no + j < tm_size)
            def _():
                defect_copy(it, j).start()
        for j in range(tm_size - 1, 0, -1):
            @pl.when(slice_no >= j)
            def _():
                defect_copy(it, j).wait_recv()
        arrived = jnp.concatenate([come[it, j] for j in range(1, tm_size - 1)], axis=1)
        total = halves(jnp.dot(arrived, stacked[...], preferred_element_type=F32))
        fresh = first[...] + come[it, 0].astype(F32) + total
        state[...] = fresh

        @pl.when(it == 0)
        def _():
            sent[1] = fresh.astype(BF)
            for d in offsets:
                @pl.when(has(d))
                def _():
                    halo_copy(1, d).start()

        return 0

    lax.fori_loop(0, ITERS, iteration, 0)
    out[...] = out[...] + exact_dot(state[...], inverse[...])

    for d in offsets:
        @pl.when(has(d))
        def _():
            meta_copy(d).wait_send()
            for it in range(ITERS):
                halo_copy(it, d).wait_send()
    for j in range(1, tm_size):
        @pl.when(slice_no + j < tm_size)
        def _():
            for it in range(ITERS):
                defect_copy(it, j).wait_send()


def solution(mesh):
    tm_size, space_size = mesh.shape["tm"], mesh.shape["space"]

    def per_device(initial, inverse, coupling, neighbours, orientation, counts):
        vmem = pl.BlockSpec(memory_space=pltpu.VMEM)
        dma = pltpu.SemaphoreType.DMA

        def body(*refs):
            kernel(tm_size, space_size, *refs)

        finish = pl.pallas_call(
            body,
            out_shape=jax.ShapeDtypeStruct((ROWS, NP), F32),
            in_specs=[pl.BlockSpec(memory_space=pltpu.HBM)] * 6,
            out_specs=vmem,
            scratch_shapes=[
                pltpu.VMEM((ROWS, NP), F32),
                pltpu.VMEM((NP, NP), F32),
                pltpu.VMEM((6 * NORI * NP, NP), BF),
                pltpu.VMEM((6, ROWS), jnp.int32),
                pltpu.VMEM((6, ROWS), jnp.int32),
                pltpu.SMEM((1,), jnp.int32),
                pltpu.VMEM((tm_size * NP, NP), F32),
                pltpu.VMEM(((tm_size - 2) * NP, 2 * NP), BF),
                pltpu.VMEM((2 * NP, 2 * NP), BF),
                pltpu.VMEM((6 * NORI * NP, 2 * NP), BF),
                pltpu.VMEM((6 * NORI, EXT, NP), BF),
                pltpu.VMEM((8, NP), F32),
                pltpu.VMEM((16, 8, NP), F32),
                pltpu.VMEM((ITERS, ROWS, NP), BF),
                pltpu.VMEM((ITERS, SPAN, ROWS, NP), BF),
                pltpu.VMEM((ITERS, ROWS, NP), BF),
                pltpu.VMEM((ITERS, tm_size - 1, ROWS, NP), BF),
                pltpu.VMEM((EXT, NP), F32),
                pltpu.VMEM((EXT, NP), F32),
                pltpu.VMEM((SWEEPS - 1, EXT, NP), F32),
                pltpu.VMEM((FSTEPS, EXT, NP), F32),
                pltpu.VMEM((ROWS, NP), F32),
                pltpu.VMEM((ROWS, NP), F32),
                dma((6,)),
                dma((SPAN,)),
                dma((SPAN,)),
                dma((ITERS, SPAN)),
                dma((ITERS, SPAN)),
                dma((ITERS, tm_size - 1)),
                dma((ITERS, tm_size - 1)),
            ],
            compiler_params=pltpu.CompilerParams(
                collective_id=0, has_side_effects=True, vmem_limit_bytes=40 << 20
            ),
            name="parareal",
        )(
            initial,
            inverse,
            coupling.reshape(6 * NORI * NP, NP),
            neighbours.T,
            orientation.T,
            counts,
        )
        return finish[None]

    return jax.shard_map(
        per_device,
        mesh=mesh,
        in_specs=(P("space", None), P(), P(), P("space", None), P("space", None), P("tm")),
        out_specs=P("tm", "space", None),
        check_vma=False,
    )
```

```python
import jax
import jax.numpy as jnp
from jax import lax
from jax.experimental import pallas as pl
from jax.experimental.pallas import tpu as pltpu
from jax.sharding import PartitionSpec as P

NP = 128
NORI = 3
FSTEPS = 4
SWEEPS = 3
ITERS = 2
FL = 32
ROWS = 64
DEPTH = FSTEPS * SWEEPS * FL // ROWS
SPAN = 2 * DEPTH + 1
EXT = SPAN * ROWS
MESSAGE = ROWS + 16
OWN = DEPTH * ROWS
SHIFTS = (-1, 1, -4, 4, -FL, FL)
MESH = pl.DeviceIdType.MESH
BF = jnp.bfloat16
F32 = jnp.float32


def row_blocks(low, high):
    units = (high - low) // 16
    count = -(-units // 16)
    cuts = [low + 16 * (units * i // count) for i in range(count + 1)]
    return [(a, b - a) for a, b in zip(cuts[:-1], cuts[1:])]


def split(values):
    head = values.astype(BF)
    return head, (values - head.astype(F32)).astype(BF)


def exact_dot(values, matrix):
    return jnp.dot(values, matrix, precision=lax.Precision.HIGHEST, preferred_element_type=F32)


def halves(product):
    return product[:, :NP] + product[:, NP:]


def kernel(
    tm_size, space_size,
    initial_hbm, inverse_hbm, coupling_hbm, neighbours_hbm, orientation_hbm, counts, out,
    initial, inverse, coupling, neighbours, orientation,
    powers, stacked, inverse_pair, weights, mask, codes, sent, halo, gone, come,
    current, following, iterate, coarse, state, first, ending,
    load_done, halo_send, halo_recv, come_send, come_recv,
):
    here = lax.axis_index("space")
    slice_no = lax.axis_index("tm")
    offsets = [d for k in range(DEPTH, 0, -1) for d in (-k, k)]
    near = offsets[::-1]
    distances = sorted(range(1, tm_size), key=lambda j: abs(j - tm_size // 2))

    def at_space(by):
        return {"space": lax.rem(here + (by + space_size), space_size)}

    def at_tm(by):
        return {"tm": lax.rem(slice_no + (by + tm_size), tm_size)}

    def has(by):
        return here + by >= 0 if by < 0 else here + by < space_size

    barrier = pltpu.get_barrier_semaphore()
    for d in offsets:
        @pl.when(has(d))
        def _():
            pl.semaphore_signal(barrier, inc=1, device_id=at_space(d), device_id_type=MESH)
    for j in range(tm_size - 1, 0, -1):
        @pl.when(slice_no >= j)
        def _():
            pl.semaphore_signal(barrier, inc=1, device_id=at_tm(-j), device_id_type=MESH)

    loads = [
        pltpu.make_async_copy(source, target, load_done.at[i])
        for i, (source, target) in enumerate((
            (neighbours_hbm, neighbours),
            (orientation_hbm, orientation),
            (inverse_hbm, inverse),
            (initial_hbm, initial),
            (coupling_hbm, coupling),
        ))
    ]
    for load in loads:
        load.start()

    def halo_copy(it, d):
        lines = pl.ds(0, MESSAGE if it == 0 else ROWS)
        return pltpu.make_async_remote_copy(
            src_ref=sent.at[it, lines], dst_ref=halo.at[it, DEPTH - d, lines],
            send_sem=halo_send.at[it, DEPTH - d], recv_sem=halo_recv.at[it, DEPTH - d],
            device_id=at_space(d), device_id_type=MESH,
        )

    def defect_copy(it, j):
        return pltpu.make_async_remote_copy(
            src_ref=gone.at[it], dst_ref=come.at[it, j - 1],
            send_sem=come_send.at[it, j - 1], recv_sem=come_recv.at[it, j - 1],
            device_id=at_tm(j), device_id_type=MESH,
        )

    for j in range(1, tm_size):
        @pl.when(slice_no < j)
        def _():
            come[:, j - 1] = jnp.zeros((ITERS, ROWS, NP), BF)
    for d in offsets:
        @pl.when(jnp.logical_not(has(d)))
        def _():
            halo[:, DEPTH + d] = jnp.zeros((ITERS, MESSAGE, NP), BF)

    loads[0].wait()
    loads[1].wait()
    found = neighbours[...]
    place = found + here * ROWS
    usable = (found >= 0) & (place >= FL) & (place < space_size * ROWS + FL)
    codes[...] = jnp.zeros_like(codes)
    codes[:6, :ROWS] = jnp.where(usable, orientation[...], NORI).astype(F32)
    sent[0, ROWS:] = codes[...].astype(BF)

    rows = lax.broadcasted_iota(jnp.int32, (NP, NP), 0)
    columns = lax.broadcasted_iota(jnp.int32, (NP, NP), 1)
    loads[2].wait()
    powers[:NP] = (rows == columns).astype(F32)
    powers[NP : 2 * NP] = inverse[...]
    known = 1
    while known < tm_size - 1:
        more = min(known, tm_size - 1 - known)
        last = powers[known * NP : (known + 1) * NP]
        powers[(known + 1) * NP : (known + 1 + more) * NP] = exact_dot(
            powers[NP : (1 + more) * NP], last
        )
        known += more
    mine = powers[pl.ds(pl.multiple_of(slice_no * NP, NP), NP)]
    loads[3].wait()
    first[...] = exact_dot(initial[...], mine)
    state[...] = first[...]
    sent[0, :ROWS] = first[...].astype(BF)

    peers = (
        jnp.minimum(here, DEPTH) + jnp.minimum(space_size - 1 - here, DEPTH) + tm_size - 1 - slice_no
    )
    pl.semaphore_wait(barrier, peers)
    for d in offsets:
        @pl.when(has(d))
        def _():
            halo_copy(0, d).start()

    head, tail = split(inverse[...])
    inverse_pair[:NP, :NP] = head
    inverse_pair[NP:, :NP] = head
    inverse_pair[:NP, NP:] = tail
    inverse_pair[NP:, NP:] = jnp.zeros_like(tail)
    for j in range(1, tm_size):
        lines = pl.ds((j - 1) * NP, NP)
        head, tail = split(powers[j * NP : (j + 1) * NP])
        stacked[lines, :NP] = head
        stacked[lines, NP:] = tail
    ending[...] = exact_dot(first[...], inverse[...])
    loads[4].wait()
    for part in range(6 * NORI):
        lines = pl.ds(part * NP, NP)
        folded = halves(
            jnp.dot(coupling[lines], inverse_pair[:NP], preferred_element_type=F32)
        )
        head, tail = split(folded)
        weights[lines, :NP] = head
        weights[lines, NP:] = tail

    def await_halo(it):
        for d in near:
            @pl.when(has(d))
            def _():
                halo_copy(it, -d).wait_recv()

    await_halo(0)
    own_codes = sent[0, ROWS:]
    gathered = [own_codes if p == DEPTH else halo[0, p, ROWS:] for p in range(SPAN)]
    gathered = [block.astype(F32)[:8] for block in gathered]
    turned = jnp.transpose(
        jnp.concatenate(gathered + [jnp.zeros((NP - 8 * SPAN, NP), F32)], axis=0)
    )
    for place_no in range(SPAN):
        for face in range(6):
            column = place_no * 8 + face
            code = jnp.broadcast_to(turned[:ROWS, column : column + 1], (ROWS, NP)).astype(BF)
            for kind in range(NORI):
                mask[face * NORI + kind, place_no * ROWS : (place_no + 1) * ROWS] = jnp.where(
                    code == jnp.array(kind, BF), jnp.array(1, BF), jnp.array(0, BF)
                )

    steps_here = counts[0]

    def iteration(it, _):
        for place_no in range(SPAN):
            lines = pl.ds(place_no * ROWS, ROWS)
            if place_no == DEPTH:
                current[lines] = state[...]
            else:
                current[lines] = halo[it, place_no, :ROWS].astype(F32)
        now, later = current, following
        for step in range(FSTEPS):
            for sweep in range(SWEEPS):
                reach = FL * (step * SWEEPS + sweep + 1)
                source = now if sweep == 0 else iterate.at[sweep - 1]
                for low, height in row_blocks(reach, EXT - reach):
                    lines = pl.ds(low, height)
                    picked = []
                    for face, shift in enumerate(SHIFTS):
                        rounded = source[pl.ds(low + shift, height)].astype(BF)
                        for kind in range(NORI):
                            picked.append(rounded * mask[face * NORI + kind, lines])
                    coupled = sum(
                        halves(
                            jnp.dot(
                                jnp.concatenate(picked[part : part + 2], axis=1),
                                weights[part * NP : (part + 2) * NP],
                                preferred_element_type=F32,
                            )
                        )
                        for part in range(0, 6 * NORI, 2)
                    )
                    if sweep == 0:
                        ahead = halves(
                            jnp.dot(
                                jnp.concatenate(split(now[lines]), axis=1),
                                inverse_pair[...],
                                preferred_element_type=F32,
                            )
                        )
                        coarse[step, lines] = ahead
                    else:
                        ahead = coarse[step, lines]
                    update = ahead - coupled
                    if sweep < SWEEPS - 1:
                        iterate[sweep, lines] = update
                    else:
                        later[lines] = jnp.where(step < steps_here, update, now[lines])
            now, later = later, now
        own = pl.ds(OWN, ROWS)
        defect = now[own] - coarse[0, own]
        out[...] = defect
        gone[it] = defect.astype(BF)
        for j in distances:
            @pl.when(slice_no + j < tm_size)
            def _():
                defect_copy(it, j).start()
        for j in distances[::-1]:
            @pl.when(slice_no >= j)
            def _():
                defect_copy(it, j).wait_recv()

        @pl.when(it == 0)
        def _():
            arrived = jnp.concatenate([come[0, j - 1] for j in range(2, tm_size)], axis=1)
            total = jnp.dot(arrived, stacked[: (tm_size - 2) * NP], preferred_element_type=F32)
            fresh = first[...] + come[0, 0].astype(F32) + halves(total)
            state[...] = fresh
            sent[1, :ROWS] = fresh.astype(BF)
            for d in offsets:
                @pl.when(has(d))
                def _():
                    halo_copy(1, d).start()
            await_halo(1)

        return 0

    lax.fori_loop(0, ITERS, iteration, 0)
    arrived = jnp.concatenate([come[1, j - 1] for j in range(1, tm_size)], axis=1)
    total = jnp.dot(arrived, stacked[...], preferred_element_type=F32)
    out[...] = out[...] + ending[...] + halves(total)

    for d in offsets:
        @pl.when(has(d))
        def _():
            for it in range(ITERS):
                halo_copy(it, d).wait_send()
    for j in range(1, tm_size):
        @pl.when(slice_no + j < tm_size)
        def _():
            for it in range(ITERS):
                defect_copy(it, j).wait_send()


def solution(mesh):
    tm_size, space_size = mesh.shape["tm"], mesh.shape["space"]

    def per_device(initial, inverse, coupling, neighbours, orientation, counts):
        vmem = pl.BlockSpec(memory_space=pltpu.VMEM)
        dma = pltpu.SemaphoreType.DMA

        def body(*refs):
            kernel(tm_size, space_size, *refs)

        finish = pl.pallas_call(
            body,
            out_shape=jax.ShapeDtypeStruct((ROWS, NP), F32),
            in_specs=[pl.BlockSpec(memory_space=pltpu.HBM)] * 5
            + [pl.BlockSpec(memory_space=pltpu.SMEM)],
            out_specs=vmem,
            scratch_shapes=[
                pltpu.VMEM((ROWS, NP), F32),
                pltpu.VMEM((NP, NP), F32),
                pltpu.VMEM((6 * NORI * NP, NP), BF),
                pltpu.VMEM((6, ROWS), jnp.int32),
                pltpu.VMEM((6, ROWS), jnp.int32),
                pltpu.VMEM((tm_size * NP, NP), F32),
                pltpu.VMEM(((tm_size - 1) * NP, 2 * NP), BF),
                pltpu.VMEM((2 * NP, 2 * NP), BF),
                pltpu.VMEM((6 * NORI * NP, 2 * NP), BF),
                pltpu.VMEM((6 * NORI, EXT, NP), BF),
                pltpu.VMEM((16, NP), F32),
                pltpu.VMEM((ITERS, MESSAGE, NP), BF),
                pltpu.VMEM((ITERS, SPAN, MESSAGE, NP), BF),
                pltpu.VMEM((ITERS, ROWS, NP), BF),
                pltpu.VMEM((ITERS, tm_size - 1, ROWS, NP), BF),
                pltpu.VMEM((EXT, NP), F32),
                pltpu.VMEM((EXT, NP), F32),
                pltpu.VMEM((SWEEPS - 1, EXT, NP), F32),
                pltpu.VMEM((FSTEPS, EXT, NP), F32),
                pltpu.VMEM((ROWS, NP), F32),
                pltpu.VMEM((ROWS, NP), F32),
                pltpu.VMEM((ROWS, NP), F32),
                dma((5,)),
                dma((ITERS, SPAN)),
                dma((ITERS, SPAN)),
                dma((ITERS, tm_size - 1)),
                dma((ITERS, tm_size - 1)),
            ],
            compiler_params=pltpu.CompilerParams(
                collective_id=0, has_side_effects=True, vmem_limit_bytes=40 << 20
            ),
            name="parareal",
        )(
            *(
                pltpu.with_memory_space_constraint(array, pltpu.HBM)
                for array in (
                    initial,
                    inverse,
                    coupling.reshape(6 * NORI * NP, NP),
                    neighbours.T,
                    orientation.T,
                )
            ),
            counts,
        )
        return finish[None]

    return jax.shard_map(
        per_device,
        mesh=mesh,
        in_specs=(P("space", None), P(), P(), P("space", None), P("space", None), P("tm")),
        out_specs=P("tm", "space", None),
        check_vma=False,
    )
```

```python
import jax
import jax.numpy as jnp
from jax import lax
from jax.experimental import pallas as pl
from jax.experimental.pallas import tpu as pltpu
from jax.sharding import PartitionSpec as P

NP = 128
NORI = 3
FSTEPS = 4
SWEEPS = 3
ITERS = 2
FL = 32
ROWS = 64
GROUP = 4
DEPTH = FSTEPS * SWEEPS * FL // ROWS
SPAN = 2 * DEPTH + 1
EXT = SPAN * ROWS
MESSAGE = ROWS + 16
OWN = DEPTH * ROWS
SHIFTS = (-1, 1, -4, 4, -FL, FL)
MESH = pl.DeviceIdType.MESH
BF = jnp.bfloat16
F32 = jnp.float32


def row_blocks(low, high):
    units = (high - low) // 16
    count = -(-units // 16)
    cuts = [low + 16 * (units * i // count) for i in range(count + 1)]
    return [(a, b - a) for a, b in zip(cuts[:-1], cuts[1:])]


def split(values):
    head = values.astype(BF)
    return head, (values - head.astype(F32)).astype(BF)


def exact_dot(values, matrix):
    return jnp.dot(values, matrix, precision=lax.Precision.HIGHEST, preferred_element_type=F32)


def halves(product):
    return product[:, :NP] + product[:, NP:]


def kernel(
    tm_size, space_size,
    initial_hbm, inverse_hbm, coupling_hbm, neighbours_hbm, orientation_hbm, counts, out,
    initial, inverse, coupling, neighbours, orientation,
    powers, gather, inside, across, inverse_pair, weights, mask, codes, sent, halo,
    gone, come, sums, older,
    current, following, iterate, coarse, state, first, ending,
    load_done, halo_send, halo_recv, come_send, come_recv, older_send, older_recv,
):
    here = lax.axis_index("space")
    slice_no = lax.axis_index("tm")
    offsets = [d for k in range(DEPTH, 0, -1) for d in (-k, k)]
    near = offsets[::-1]
    groups = tm_size // GROUP
    group, lane = slice_no // GROUP, lax.rem(slice_no, GROUP)
    lanes = (
        lane,
        lane + 1 - 2 * lax.rem(lane, 2),
        lane + 2 - 4 * (lane // 2),
        GROUP - 1 - lane,
    )

    def at_space(by):
        return {"space": lax.rem(here + (by + space_size), space_size)}

    def at_lane(k):
        return {"tm": group * GROUP + lanes[k]}

    def at_group(by):
        return {"tm": lax.rem(slice_no + (by * GROUP + tm_size), tm_size)}

    def has(by):
        return here + by >= 0 if by < 0 else here + by < space_size

    barrier = pltpu.get_barrier_semaphore()
    for d in offsets:
        @pl.when(has(d))
        def _():
            pl.semaphore_signal(barrier, inc=1, device_id=at_space(d), device_id_type=MESH)
    for k in range(groups - 1, 0, -1):
        @pl.when(group >= k)
        def _():
            pl.semaphore_signal(barrier, inc=1, device_id=at_group(-k), device_id_type=MESH)
    for k in range(1, GROUP):
        pl.semaphore_signal(barrier, inc=1, device_id=at_lane(k), device_id_type=MESH)

    loads = [
        pltpu.make_async_copy(source, target, load_done.at[i])
        for i, (source, target) in enumerate((
            (neighbours_hbm, neighbours),
            (orientation_hbm, orientation),
            (inverse_hbm, inverse),
            (initial_hbm, initial),
            (coupling_hbm, coupling),
        ))
    ]
    for load in loads:
        load.start()

    def halo_copy(it, d):
        lines = pl.ds(0, MESSAGE if it == 0 else ROWS)
        return pltpu.make_async_remote_copy(
            src_ref=sent.at[it, lines], dst_ref=halo.at[it, DEPTH - d, lines],
            send_sem=halo_send.at[it, DEPTH - d], recv_sem=halo_recv.at[it, DEPTH - d],
            device_id=at_space(d), device_id_type=MESH,
        )

    def defect_copy(it, k):
        return pltpu.make_async_remote_copy(
            src_ref=gone.at[it], dst_ref=come.at[it, k - 1],
            send_sem=come_send.at[it, k - 1], recv_sem=come_recv.at[it, k - 1],
            device_id=at_lane(k), device_id_type=MESH,
        )

    def sum_copy(it, k):
        return pltpu.make_async_remote_copy(
            src_ref=sums.at[it], dst_ref=older.at[it, k - 1],
            send_sem=older_send.at[it, k - 1], recv_sem=older_recv.at[it, k - 1],
            device_id=at_group(k), device_id_type=MESH,
        )

    for k in range(1, groups):
        @pl.when(group < k)
        def _():
            older[:, k - 1] = jnp.zeros((ITERS, ROWS, NP), BF)
    for d in offsets:
        @pl.when(jnp.logical_not(has(d)))
        def _():
            halo[:, DEPTH + d] = jnp.zeros((ITERS, MESSAGE, NP), BF)

    loads[0].wait()
    loads[1].wait()
    found = neighbours[...]
    place = found + here * ROWS
    usable = (found >= 0) & (place >= FL) & (place < space_size * ROWS + FL)
    codes[...] = jnp.zeros_like(codes)
    codes[:6, :ROWS] = jnp.where(usable, orientation[...], NORI).astype(F32)
    sent[0, ROWS:] = codes[...].astype(BF)

    rows = lax.broadcasted_iota(jnp.int32, (NP, NP), 0)
    columns = lax.broadcasted_iota(jnp.int32, (NP, NP), 1)
    loads[2].wait()
    powers[:NP] = (rows == columns).astype(F32)
    powers[NP : 2 * NP] = inverse[...]
    known = 1
    while known < tm_size - 1:
        more = min(known, tm_size - 1 - known)
        last = powers[known * NP : (known + 1) * NP]
        powers[(known + 1) * NP : (known + 1 + more) * NP] = exact_dot(
            powers[NP : (1 + more) * NP], last
        )
        known += more
    mine = powers[pl.ds(pl.multiple_of(slice_no * NP, NP), NP)]
    loads[3].wait()
    first[...] = exact_dot(initial[...], mine)
    state[...] = first[...]
    sent[0, :ROWS] = first[...].astype(BF)

    peers = (
        jnp.minimum(here, DEPTH) + jnp.minimum(space_size - 1 - here, DEPTH)
        + GROUP - 1 + groups - 1 - group
    )
    pl.semaphore_wait(barrier, peers)
    for d in offsets:
        @pl.when(has(d))
        def _():
            halo_copy(0, d).start()

    head, tail = split(inverse[...])
    inverse_pair[:NP, :NP] = head
    inverse_pair[NP:, :NP] = head
    inverse_pair[:NP, NP:] = tail
    inverse_pair[NP:, NP:] = jnp.zeros_like(tail)
    def power_pair(exponent):
        line = pl.multiple_of(jnp.maximum(exponent, 0) * NP, NP)
        power = jnp.where(exponent >= 0, powers[pl.ds(line, NP)], 0.0)
        return jnp.concatenate(split(power), axis=1)

    for k in range(GROUP):
        gather[k * NP : (k + 1) * NP] = power_pair(GROUP - 1 - lanes[k])
    for it in range(ITERS):
        for k in range(1, GROUP):
            ahead = lane - lanes[k]
            inside[it, (k - 1) * NP : k * NP] = power_pair(
                jnp.where(ahead > 0, ahead - 1 + it, -1)
            )
        for k in range(1, groups):
            across[it, (k - 1) * NP : k * NP] = power_pair(GROUP * (k - 1) + lane + it)
    ending[...] = exact_dot(first[...], inverse[...])
    loads[4].wait()
    for part in range(6 * NORI):
        lines = pl.ds(part * NP, NP)
        folded = halves(
            jnp.dot(coupling[lines], inverse_pair[:NP], preferred_element_type=F32)
        )
        head, tail = split(folded)
        weights[lines, :NP] = head
        weights[lines, NP:] = tail

    def await_halo(it):
        for d in near:
            @pl.when(has(d))
            def _():
                halo_copy(it, -d).wait_recv()

    await_halo(0)
    own_codes = sent[0, ROWS:]
    gathered = [own_codes if p == DEPTH else halo[0, p, ROWS:] for p in range(SPAN)]
    gathered = [block.astype(F32)[:8] for block in gathered]
    turned = jnp.transpose(
        jnp.concatenate(gathered + [jnp.zeros((NP - 8 * SPAN, NP), F32)], axis=0)
    )
    for place_no in range(SPAN):
        for face in range(6):
            column = place_no * 8 + face
            code = jnp.broadcast_to(turned[:ROWS, column : column + 1], (ROWS, NP)).astype(BF)
            for kind in range(NORI):
                mask[face * NORI + kind, place_no * ROWS : (place_no + 1) * ROWS] = jnp.where(
                    code == jnp.array(kind, BF), jnp.array(1, BF), jnp.array(0, BF)
                )

    steps_here = counts[0]

    def iteration(it, _):
        for place_no in range(SPAN):
            lines = pl.ds(place_no * ROWS, ROWS)
            if place_no == DEPTH:
                current[lines] = state[...]
            else:
                current[lines] = halo[it, place_no, :ROWS].astype(F32)
        now, later = current, following
        for step in range(FSTEPS):
            for sweep in range(SWEEPS):
                reach = FL * (step * SWEEPS + sweep + 1)
                source = now if sweep == 0 else iterate.at[sweep - 1]
                for low, height in row_blocks(reach, EXT - reach):
                    lines = pl.ds(low, height)
                    picked = []
                    for face, shift in enumerate(SHIFTS):
                        rounded = source[pl.ds(low + shift, height)].astype(BF)
                        for kind in range(NORI):
                            picked.append(rounded * mask[face * NORI + kind, lines])
                    coupled = sum(
                        halves(
                            jnp.dot(
                                jnp.concatenate(picked[part : part + 2], axis=1),
                                weights[part * NP : (part + 2) * NP],
                                preferred_element_type=F32,
                            )
                        )
                        for part in range(0, 6 * NORI, 2)
                    )
                    if sweep == 0:
                        ahead = halves(
                            jnp.dot(
                                jnp.concatenate(split(now[lines]), axis=1),
                                inverse_pair[...],
                                preferred_element_type=F32,
                            )
                        )
                        coarse[step, lines] = ahead
                    else:
                        ahead = coarse[step, lines]
                    update = ahead - coupled
                    if sweep < SWEEPS - 1:
                        iterate[sweep, lines] = update
                    else:
                        later[lines] = jnp.where(step < steps_here, update, now[lines])
            now, later = later, now
        own = pl.ds(OWN, ROWS)
        defect = now[own] - coarse[0, own]
        gone[it] = defect.astype(BF)
        for k in range(GROUP - 1, 0, -1):
            defect_copy(it, k).start()
        for k in range(1, GROUP):
            defect_copy(it, k).wait_recv()
        group_defects = jnp.concatenate([gone[it], *(come[it, k] for k in range(GROUP - 1))], axis=1)
        sums[it] = halves(
            jnp.dot(group_defects, gather[...], preferred_element_type=F32)
        ).astype(BF)
        for k in (2, 3, 1):
            @pl.when(group + k < groups)
            def _():
                sum_copy(it, k).start()
        change = halves(
            jnp.dot(group_defects[:, NP:], inside[it], preferred_element_type=F32)
        )
        for k in (1, 3, 2):
            @pl.when(group >= k)
            def _():
                sum_copy(it, k).wait_recv()
        change += halves(
            jnp.dot(
                jnp.concatenate([older[it, k] for k in range(groups - 1)], axis=1),
                across[it],
                preferred_element_type=F32,
            )
        )

        @pl.when(it == 0)
        def _():
            fresh = first[...] + change
            state[...] = fresh
            sent[1, :ROWS] = fresh.astype(BF)
            for d in offsets:
                @pl.when(has(d))
                def _():
                    halo_copy(1, d).start()
            await_halo(1)

        @pl.when(it == ITERS - 1)
        def _():
            out[...] = ending[...] + defect + change

        return 0

    lax.fori_loop(0, ITERS, iteration, 0)

    for d in offsets:
        @pl.when(has(d))
        def _():
            for it in range(ITERS):
                halo_copy(it, d).wait_send()
    for it in range(ITERS):
        for k in range(1, GROUP):
            defect_copy(it, k).wait_send()
    for k in range(1, groups):
        @pl.when(group + k < groups)
        def _():
            for it in range(ITERS):
                sum_copy(it, k).wait_send()


def solution(mesh):
    tm_size, space_size = mesh.shape["tm"], mesh.shape["space"]
    groups = tm_size // GROUP

    def per_device(initial, inverse, coupling, neighbours, orientation, counts):
        vmem = pl.BlockSpec(memory_space=pltpu.VMEM)
        dma = pltpu.SemaphoreType.DMA

        def body(*refs):
            kernel(tm_size, space_size, *refs)

        finish = pl.pallas_call(
            body,
            out_shape=jax.ShapeDtypeStruct((ROWS, NP), F32),
            in_specs=[pl.BlockSpec(memory_space=pltpu.HBM)] * 5
            + [pl.BlockSpec(memory_space=pltpu.SMEM)],
            out_specs=vmem,
            scratch_shapes=[
                pltpu.VMEM((ROWS, NP), F32),
                pltpu.VMEM((NP, NP), F32),
                pltpu.VMEM((6 * NORI * NP, NP), BF),
                pltpu.VMEM((6, ROWS), jnp.int32),
                pltpu.VMEM((6, ROWS), jnp.int32),
                pltpu.VMEM((tm_size * NP, NP), F32),
                pltpu.VMEM((GROUP * NP, 2 * NP), BF),
                pltpu.VMEM((ITERS, (GROUP - 1) * NP, 2 * NP), BF),
                pltpu.VMEM((ITERS, (groups - 1) * NP, 2 * NP), BF),
                pltpu.VMEM((2 * NP, 2 * NP), BF),
                pltpu.VMEM((6 * NORI * NP, 2 * NP), BF),
                pltpu.VMEM((6 * NORI, EXT, NP), BF),
                pltpu.VMEM((16, NP), F32),
                pltpu.VMEM((ITERS, MESSAGE, NP), BF),
                pltpu.VMEM((ITERS, SPAN, MESSAGE, NP), BF),
                pltpu.VMEM((ITERS, ROWS, NP), BF),
                pltpu.VMEM((ITERS, GROUP - 1, ROWS, NP), BF),
                pltpu.VMEM((ITERS, ROWS, NP), BF),
                pltpu.VMEM((ITERS, groups - 1, ROWS, NP), BF),
                pltpu.VMEM((EXT, NP), F32),
                pltpu.VMEM((EXT, NP), F32),
                pltpu.VMEM((SWEEPS - 1, EXT, NP), F32),
                pltpu.VMEM((FSTEPS, EXT, NP), F32),
                pltpu.VMEM((ROWS, NP), F32),
                pltpu.VMEM((ROWS, NP), F32),
                pltpu.VMEM((ROWS, NP), F32),
                dma((5,)),
                dma((ITERS, SPAN)),
                dma((ITERS, SPAN)),
                dma((ITERS, GROUP - 1)),
                dma((ITERS, GROUP - 1)),
                dma((ITERS, groups - 1)),
                dma((ITERS, groups - 1)),
            ],
            compiler_params=pltpu.CompilerParams(
                collective_id=0, has_side_effects=True, vmem_limit_bytes=40 << 20
            ),
            name="parareal",
        )(
            *(
                pltpu.with_memory_space_constraint(array, pltpu.HBM)
                for array in (
                    initial,
                    inverse,
                    coupling.reshape(6 * NORI * NP, NP),
                    neighbours.T,
                    orientation.T,
                )
            ),
            counts,
        )
        return finish[None]

    return jax.shard_map(
        per_device,
        mesh=mesh,
        in_specs=(P("space", None), P(), P(), P("space", None), P("space", None), P("tm")),
        out_specs=P("tm", "space", None),
        check_vma=False,
    )
```

```python
import jax
import jax.numpy as jnp
from jax import lax
from jax.experimental import pallas as pl
from jax.experimental.pallas import tpu as pltpu
from jax.sharding import PartitionSpec as P

NP = 128
NORI = 3
FSTEPS = 4
SWEEPS = 3
ITERS = 2
FL = 32
ROWS = 64
GROUP = 4
DEPTH = FSTEPS * SWEEPS * FL // ROWS
SPAN = 2 * DEPTH + 1
EXT = SPAN * ROWS
MESSAGE = ROWS + 16
OWN = DEPTH * ROWS
SHIFTS = (-1, 1, -4, 4, -FL, FL)
MESH = pl.DeviceIdType.MESH
BF = jnp.bfloat16
F32 = jnp.float32


def row_blocks(low, high):
    units = (high - low) // 16
    count = -(-units // 16)
    cuts = [low + 16 * (units * i // count) for i in range(count + 1)]
    return [(a, b - a) for a, b in zip(cuts[:-1], cuts[1:])]


def split(values):
    head = values.astype(BF)
    return head, (values - head.astype(F32)).astype(BF)


def exact_dot(values, matrix):
    return jnp.dot(values, matrix, precision=lax.Precision.HIGHEST, preferred_element_type=F32)


def halves(product):
    return product[:, :NP] + product[:, NP:]


def kernel(
    tm_size, space_size,
    initial_hbm, inverse_hbm, coupling_hbm, neighbours_hbm, orientation_hbm, counts, out,
    initial, inverse, coupling, neighbours, orientation,
    powers, gather, inside, across, inverse_pair, weights, mask, codes, sent, halo,
    gone, come, sums, older,
    current, following, iterate, coarse, first, ending,
    load_done, halo_send, halo_recv, come_send, come_recv, older_send, older_recv,
):
    here = lax.axis_index("space")
    slice_no = lax.axis_index("tm")
    offsets = [d for k in range(DEPTH, 0, -1) for d in (-k, k)]
    near = offsets[::-1]
    groups = tm_size // GROUP
    group, lane = slice_no // GROUP, lax.rem(slice_no, GROUP)
    lanes = (
        lane,
        lane + 1 - 2 * lax.rem(lane, 2),
        lane + 2 - 4 * (lane // 2),
        GROUP - 1 - lane,
    )

    def at_space(by):
        return {"space": lax.rem(here + (by + space_size), space_size)}

    def at_lane(k):
        return {"tm": group * GROUP + lanes[k]}

    def at_group(by):
        return {"tm": lax.rem(slice_no + (by * GROUP + tm_size), tm_size)}

    def has(by):
        return here + by >= 0 if by < 0 else here + by < space_size

    barrier = pltpu.get_barrier_semaphore()
    for d in offsets:
        @pl.when(has(d))
        def _():
            pl.semaphore_signal(barrier, inc=1, device_id=at_space(d), device_id_type=MESH)
    for k in range(groups - 1, 0, -1):
        @pl.when(group >= k)
        def _():
            pl.semaphore_signal(barrier, inc=1, device_id=at_group(-k), device_id_type=MESH)
    for k in range(1, GROUP):
        pl.semaphore_signal(barrier, inc=1, device_id=at_lane(k), device_id_type=MESH)

    loads = [
        pltpu.make_async_copy(source, target, load_done.at[i])
        for i, (source, target) in enumerate((
            (neighbours_hbm, neighbours),
            (orientation_hbm, orientation),
            (inverse_hbm, inverse),
            (initial_hbm, initial),
            (coupling_hbm, coupling),
        ))
    ]
    for load in loads:
        load.start()

    def halo_copy(it, d):
        lines = pl.ds(0, MESSAGE if it == 0 else ROWS)
        return pltpu.make_async_remote_copy(
            src_ref=sent.at[it, lines], dst_ref=halo.at[it, DEPTH - d, lines],
            send_sem=halo_send.at[it, DEPTH - d], recv_sem=halo_recv.at[it, DEPTH - d],
            device_id=at_space(d), device_id_type=MESH,
        )

    def defect_copy(it, k):
        return pltpu.make_async_remote_copy(
            src_ref=gone.at[it], dst_ref=come.at[it, k - 1],
            send_sem=come_send.at[it, k - 1], recv_sem=come_recv.at[it, k - 1],
            device_id=at_lane(k), device_id_type=MESH,
        )

    def sum_copy(it, k):
        return pltpu.make_async_remote_copy(
            src_ref=sums.at[it], dst_ref=older.at[it, k - 1],
            send_sem=older_send.at[it, k - 1], recv_sem=older_recv.at[it, k - 1],
            device_id=at_group(k), device_id_type=MESH,
        )

    for k in range(1, groups):
        @pl.when(group < k)
        def _():
            older[:, k - 1] = jnp.zeros((ITERS, ROWS, NP), BF)
    for d in offsets:
        @pl.when(jnp.logical_not(has(d)))
        def _():
            halo[:, DEPTH + d] = jnp.zeros((ITERS, MESSAGE, NP), BF)

    loads[0].wait()
    loads[1].wait()
    found = neighbours[...]
    place = found + here * ROWS
    usable = (found >= 0) & (place >= FL) & (place < space_size * ROWS + FL)
    codes[...] = jnp.zeros_like(codes)
    codes[:6, :ROWS] = jnp.where(usable, orientation[...], NORI).astype(F32)
    sent[0, ROWS:] = codes[...].astype(BF)

    loads[3].wait()
    sent[0, :ROWS] = initial[...].astype(BF)

    peers = (
        jnp.minimum(here, DEPTH) + jnp.minimum(space_size - 1 - here, DEPTH)
        + GROUP - 1 + groups - 1 - group
    )
    pl.semaphore_wait(barrier, peers)
    for d in offsets:
        @pl.when(has(d))
        def _():
            halo_copy(0, d).start()

    rows = lax.broadcasted_iota(jnp.int32, (NP, NP), 0)
    columns = lax.broadcasted_iota(jnp.int32, (NP, NP), 1)
    loads[2].wait()
    powers[:NP] = (rows == columns).astype(F32)
    powers[NP : 2 * NP] = inverse[...]
    known = 1
    while known < tm_size - 1:
        more = min(known, tm_size - 1 - known)
        last = powers[known * NP : (known + 1) * NP]
        powers[(known + 1) * NP : (known + 1 + more) * NP] = exact_dot(
            powers[NP : (1 + more) * NP], last
        )
        known += more
    mine = powers[pl.ds(pl.multiple_of(slice_no * NP, NP), NP)]
    first[...] = exact_dot(initial[...], mine)
    mine_pair = jnp.concatenate(split(mine), axis=1)

    head, tail = split(inverse[...])
    inverse_pair[:NP, :NP] = head
    inverse_pair[NP:, :NP] = head
    inverse_pair[:NP, NP:] = tail
    inverse_pair[NP:, NP:] = jnp.zeros_like(tail)
    def power_pair(exponent):
        line = pl.multiple_of(jnp.maximum(exponent, 0) * NP, NP)
        power = jnp.where(exponent >= 0, powers[pl.ds(line, NP)], 0.0)
        return jnp.concatenate(split(power), axis=1)

    for k in range(GROUP):
        gather[k * NP : (k + 1) * NP] = power_pair(GROUP - 1 - lanes[k])
    for it in range(ITERS):
        for k in range(1, GROUP):
            ahead = lane - lanes[k]
            inside[it, (k - 1) * NP : k * NP] = power_pair(
                jnp.where(ahead > 0, ahead - 1 + it, -1)
            )
        for k in range(1, groups):
            across[it, (k - 1) * NP : k * NP] = power_pair(GROUP * (k - 1) + lane + it)
    ending[...] = exact_dot(first[...], inverse[...])
    loads[4].wait()
    for part in range(6 * NORI):
        lines = pl.ds(part * NP, NP)
        folded = halves(
            jnp.dot(coupling[lines], inverse_pair[:NP], preferred_element_type=F32)
        )
        head, tail = split(folded)
        weights[lines, :NP] = head
        weights[lines, NP:] = tail

    def await_halo(it):
        for d in near:
            @pl.when(has(d))
            def _():
                halo_copy(it, -d).wait_recv()

    await_halo(0)
    own_codes = sent[0, ROWS:]
    gathered = [own_codes if p == DEPTH else halo[0, p, ROWS:] for p in range(SPAN)]
    gathered = [block.astype(F32)[:8] for block in gathered]
    turned = jnp.transpose(
        jnp.concatenate(gathered + [jnp.zeros((NP - 8 * SPAN, NP), F32)], axis=0)
    )
    for place_no in range(SPAN):
        for face in range(6):
            column = place_no * 8 + face
            code = jnp.broadcast_to(turned[:ROWS, column : column + 1], (ROWS, NP)).astype(BF)
            for kind in range(NORI):
                mask[face * NORI + kind, place_no * ROWS : (place_no + 1) * ROWS] = jnp.where(
                    code == jnp.array(kind, BF), jnp.array(1, BF), jnp.array(0, BF)
                )

    for place_no in (0, DEPTH + 1):
        around = halo[0, place_no : place_no + DEPTH, :ROWS].reshape(DEPTH * ROWS, NP)
        current[pl.ds(place_no * ROWS, DEPTH * ROWS)] = halves(
            jnp.dot(around, mine_pair, preferred_element_type=F32)
        )
    current[pl.ds(OWN, ROWS)] = first[...]

    steps_here = counts[0]

    def iteration(it, _):
        now, later = current, following
        for step in range(FSTEPS):
            for sweep in range(SWEEPS):
                reach = FL * (step * SWEEPS + sweep + 1)
                source = now if sweep == 0 else iterate.at[sweep - 1]
                for low, height in row_blocks(reach, EXT - reach):
                    lines = pl.ds(low, height)
                    picked = []
                    for face, shift in enumerate(SHIFTS):
                        rounded = source[pl.ds(low + shift, height)].astype(BF)
                        for kind in range(NORI):
                            picked.append(rounded * mask[face * NORI + kind, lines])
                    coupled = sum(
                        halves(
                            jnp.dot(
                                jnp.concatenate(picked[part : part + 2], axis=1),
                                weights[part * NP : (part + 2) * NP],
                                preferred_element_type=F32,
                            )
                        )
                        for part in range(0, 6 * NORI, 2)
                    )
                    if sweep == 0:
                        ahead = halves(
                            jnp.dot(
                                jnp.concatenate(split(now[lines]), axis=1),
                                inverse_pair[...],
                                preferred_element_type=F32,
                            )
                        )
                        coarse[step, lines] = ahead
                    else:
                        ahead = coarse[step, lines]
                    update = ahead - coupled
                    if sweep < SWEEPS - 1:
                        iterate[sweep, lines] = update
                    else:
                        later[lines] = jnp.where(step < steps_here, update, now[lines])
            now, later = later, now
        own = pl.ds(OWN, ROWS)
        defect = now[own] - coarse[0, own]
        gone[it] = defect.astype(BF)
        for k in range(GROUP - 1, 0, -1):
            defect_copy(it, k).start()
        for k in range(1, GROUP):
            defect_copy(it, k).wait_recv()
        group_defects = jnp.concatenate([gone[it], *(come[it, k] for k in range(GROUP - 1))], axis=1)
        sums[it] = halves(
            jnp.dot(group_defects, gather[...], preferred_element_type=F32)
        ).astype(BF)
        for k in (2, 3, 1):
            @pl.when(group + k < groups)
            def _():
                sum_copy(it, k).start()
        change = halves(
            jnp.dot(group_defects[:, NP:], inside[it], preferred_element_type=F32)
        )
        for k in (1, 3, 2):
            @pl.when(group >= k)
            def _():
                sum_copy(it, k).wait_recv()
        change += halves(
            jnp.dot(
                jnp.concatenate([older[it, k] for k in range(groups - 1)], axis=1),
                across[it],
                preferred_element_type=F32,
            )
        )

        @pl.when(it == 0)
        def _():
            fresh = first[...] + change
            current[pl.ds(OWN, ROWS)] = fresh
            sent[1, :ROWS] = fresh.astype(BF)
            for d in offsets:
                @pl.when(has(d))
                def _():
                    halo_copy(1, d).start()
            await_halo(1)
            for place_no in range(SPAN):
                if place_no != DEPTH:
                    lines = pl.ds(place_no * ROWS, ROWS)
                    current[lines] = halo[1, place_no, :ROWS].astype(F32)

        @pl.when(it == ITERS - 1)
        def _():
            out[...] = ending[...] + defect + change

        return 0

    lax.fori_loop(0, ITERS, iteration, 0)

    for d in offsets:
        @pl.when(has(d))
        def _():
            for it in range(ITERS):
                halo_copy(it, d).wait_send()
    for it in range(ITERS):
        for k in range(1, GROUP):
            defect_copy(it, k).wait_send()
    for k in range(1, groups):
        @pl.when(group + k < groups)
        def _():
            for it in range(ITERS):
                sum_copy(it, k).wait_send()


def solution(mesh):
    tm_size, space_size = mesh.shape["tm"], mesh.shape["space"]
    groups = tm_size // GROUP

    def per_device(initial, inverse, coupling, neighbours, orientation, counts):
        vmem = pl.BlockSpec(memory_space=pltpu.VMEM)
        dma = pltpu.SemaphoreType.DMA

        def body(*refs):
            kernel(tm_size, space_size, *refs)

        finish = pl.pallas_call(
            body,
            out_shape=jax.ShapeDtypeStruct((ROWS, NP), F32),
            in_specs=[pl.BlockSpec(memory_space=pltpu.HBM)] * 5
            + [pl.BlockSpec(memory_space=pltpu.SMEM)],
            out_specs=vmem,
            scratch_shapes=[
                pltpu.VMEM((ROWS, NP), F32),
                pltpu.VMEM((NP, NP), F32),
                pltpu.VMEM((6 * NORI * NP, NP), BF),
                pltpu.VMEM((6, ROWS), jnp.int32),
                pltpu.VMEM((6, ROWS), jnp.int32),
                pltpu.VMEM((tm_size * NP, NP), F32),
                pltpu.VMEM((GROUP * NP, 2 * NP), BF),
                pltpu.VMEM((ITERS, (GROUP - 1) * NP, 2 * NP), BF),
                pltpu.VMEM((ITERS, (groups - 1) * NP, 2 * NP), BF),
                pltpu.VMEM((2 * NP, 2 * NP), BF),
                pltpu.VMEM((6 * NORI * NP, 2 * NP), BF),
                pltpu.VMEM((6 * NORI, EXT, NP), BF),
                pltpu.VMEM((16, NP), F32),
                pltpu.VMEM((ITERS, MESSAGE, NP), BF),
                pltpu.VMEM((ITERS, SPAN, MESSAGE, NP), BF),
                pltpu.VMEM((ITERS, ROWS, NP), BF),
                pltpu.VMEM((ITERS, GROUP - 1, ROWS, NP), BF),
                pltpu.VMEM((ITERS, ROWS, NP), BF),
                pltpu.VMEM((ITERS, groups - 1, ROWS, NP), BF),
                pltpu.VMEM((EXT, NP), F32),
                pltpu.VMEM((EXT, NP), F32),
                pltpu.VMEM((SWEEPS - 1, EXT, NP), F32),
                pltpu.VMEM((FSTEPS, EXT, NP), F32),
                pltpu.VMEM((ROWS, NP), F32),
                pltpu.VMEM((ROWS, NP), F32),
                dma((5,)),
                dma((ITERS, SPAN)),
                dma((ITERS, SPAN)),
                dma((ITERS, GROUP - 1)),
                dma((ITERS, GROUP - 1)),
                dma((ITERS, groups - 1)),
                dma((ITERS, groups - 1)),
            ],
            compiler_params=pltpu.CompilerParams(
                collective_id=0, has_side_effects=True, vmem_limit_bytes=40 << 20
            ),
            name="parareal",
        )(
            *(
                pltpu.with_memory_space_constraint(array, pltpu.HBM)
                for array in (
                    initial,
                    inverse,
                    coupling.reshape(6 * NORI * NP, NP),
                    neighbours.T,
                    orientation.T,
                )
            ),
            counts,
        )
        return finish[None]

    return jax.shard_map(
        per_device,
        mesh=mesh,
        in_specs=(P("space", None), P(), P(), P("space", None), P("space", None), P("tm")),
        out_specs=P("tm", "space", None),
        check_vma=False,
    )
```

```python
import jax
import jax.numpy as jnp
from jax import lax
from jax.experimental import pallas as pl
from jax.experimental.pallas import tpu as pltpu
from jax.sharding import PartitionSpec as P

NP = 128
NORI = 3
FSTEPS = 4
SWEEPS = 3
ITERS = 2
FL = 32
ROWS = 64
GROUP = 4
DEPTH = FSTEPS * SWEEPS * FL // ROWS
SPAN = 2 * DEPTH + 1
EXT = SPAN * ROWS
MESSAGE = ROWS + 16
OWN = DEPTH * ROWS
SHIFTS = (-1, 1, -4, 4, -FL, FL)
MESH = pl.DeviceIdType.MESH
BF = jnp.bfloat16
F32 = jnp.float32


def row_blocks(low, high):
    units = (high - low) // 16
    count = -(-units // 16)
    cuts = [low + 16 * (units * i // count) for i in range(count + 1)]
    return [(a, b - a) for a, b in zip(cuts[:-1], cuts[1:])]


def split(values):
    head = values.astype(BF)
    return head, (values - head.astype(F32)).astype(BF)


def exact_dot(values, matrix):
    return jnp.dot(values, matrix, precision=lax.Precision.HIGHEST, preferred_element_type=F32)


def halves(product):
    return product[:, :NP] + product[:, NP:]


def kernel(
    tm_size, space_size,
    initial_hbm, inverse_hbm, coupling_hbm, neighbours_hbm, orientation_hbm, counts, out,
    initial, inverse, coupling, neighbours, orientation,
    powers, own_power, gather, inside, across, inverse_pair, weights, mask, codes, sent, halo,
    gone, come, sums, older,
    current, following, iterate, coarse, state, first, ending,
    load_done, halo_send, halo_recv, come_send, come_recv, older_send, older_recv,
):
    here = lax.axis_index("space")
    slice_no = lax.axis_index("tm")
    offsets = [d for k in range(DEPTH, 0, -1) for d in (-k, k)]
    near = offsets[::-1]
    groups = tm_size // GROUP
    group, lane = slice_no // GROUP, lax.rem(slice_no, GROUP)
    lanes = (
        lane,
        lane + 1 - 2 * lax.rem(lane, 2),
        lane + 2 - 4 * (lane // 2),
        GROUP - 1 - lane,
    )

    def at_space(by):
        return {"space": lax.rem(here + (by + space_size), space_size)}

    def at_lane(k):
        return {"tm": group * GROUP + lanes[k]}

    def at_group(by):
        return {"tm": lax.rem(slice_no + (by * GROUP + tm_size), tm_size)}

    def has(by):
        return here + by >= 0 if by < 0 else here + by < space_size

    barrier = pltpu.get_barrier_semaphore()
    for d in offsets:
        @pl.when(has(d))
        def _():
            pl.semaphore_signal(barrier, inc=1, device_id=at_space(d), device_id_type=MESH)
    for k in range(groups - 1, 0, -1):
        @pl.when(group >= k)
        def _():
            pl.semaphore_signal(barrier, inc=1, device_id=at_group(-k), device_id_type=MESH)
    for k in range(1, GROUP):
        pl.semaphore_signal(barrier, inc=1, device_id=at_lane(k), device_id_type=MESH)

    loads = [
        pltpu.make_async_copy(source, target, load_done.at[i])
        for i, (source, target) in enumerate((
            (neighbours_hbm, neighbours),
            (orientation_hbm, orientation),
            (inverse_hbm, inverse),
            (initial_hbm, initial),
            (coupling_hbm, coupling),
        ))
    ]
    for load in loads:
        load.start()

    def halo_copy(it, d):
        lines = pl.ds(0, MESSAGE if it == 0 else ROWS)
        return pltpu.make_async_remote_copy(
            src_ref=sent.at[it, lines], dst_ref=halo.at[it, DEPTH - d, lines],
            send_sem=halo_send.at[it, DEPTH - d], recv_sem=halo_recv.at[it, DEPTH - d],
            device_id=at_space(d), device_id_type=MESH,
        )

    def defect_copy(it, k):
        return pltpu.make_async_remote_copy(
            src_ref=gone.at[it], dst_ref=come.at[it, k - 1],
            send_sem=come_send.at[it, k - 1], recv_sem=come_recv.at[it, k - 1],
            device_id=at_lane(k), device_id_type=MESH,
        )

    def sum_copy(it, k):
        return pltpu.make_async_remote_copy(
            src_ref=sums.at[it], dst_ref=older.at[it, k - 1],
            send_sem=older_send.at[it, k - 1], recv_sem=older_recv.at[it, k - 1],
            device_id=at_group(k), device_id_type=MESH,
        )

    for k in range(1, groups):
        @pl.when(group < k)
        def _():
            older[:, k - 1] = jnp.zeros((ITERS, ROWS, NP), BF)
    for d in offsets:
        @pl.when(jnp.logical_not(has(d)))
        def _():
            halo[:, DEPTH + d] = jnp.zeros((ITERS, MESSAGE, NP), BF)

    loads[0].wait()
    loads[1].wait()
    found = neighbours[...]
    place = found + here * ROWS
    usable = (found >= 0) & (place >= FL) & (place < space_size * ROWS + FL)
    codes[...] = jnp.zeros_like(codes)
    codes[:6, :ROWS] = jnp.where(usable, orientation[...], NORI).astype(F32)
    sent[0, ROWS:] = codes[...].astype(BF)

    rows = lax.broadcasted_iota(jnp.int32, (NP, NP), 0)
    columns = lax.broadcasted_iota(jnp.int32, (NP, NP), 1)
    loads[2].wait()
    powers[:NP] = (rows == columns).astype(F32)
    powers[NP : 2 * NP] = inverse[...]
    known = 1
    while known < tm_size - 1:
        more = min(known, tm_size - 1 - known)
        last = powers[known * NP : (known + 1) * NP]
        powers[(known + 1) * NP : (known + 1 + more) * NP] = exact_dot(
            powers[NP : (1 + more) * NP], last
        )
        known += more
    mine = powers[pl.ds(pl.multiple_of(slice_no * NP, NP), NP)]
    loads[3].wait()
    first[...] = exact_dot(initial[...], mine)
    state[...] = first[...]
    sent[0, :ROWS] = first[...].astype(BF)

    peers = (
        jnp.minimum(here, DEPTH) + jnp.minimum(space_size - 1 - here, DEPTH)
        + GROUP - 1 + groups - 1 - group
    )
    pl.semaphore_wait(barrier, peers)
    for d in offsets:
        @pl.when(has(d))
        def _():
            halo_copy(0, d).start()

    head, tail = split(inverse[...])
    inverse_pair[:NP, :NP] = head
    inverse_pair[NP:, :NP] = head
    inverse_pair[:NP, NP:] = tail
    inverse_pair[NP:, NP:] = jnp.zeros_like(tail)
    def power_pair(exponent):
        line = pl.multiple_of(jnp.maximum(exponent, 0) * NP, NP)
        power = jnp.where(exponent >= 0, powers[pl.ds(line, NP)], 0.0)
        return jnp.concatenate(split(power), axis=1)

    pair = power_pair(GROUP - 1 - lane)
    own_power[:NP] = pair
    own_power[NP:, :NP] = pair[:, :NP]
    own_power[NP:, NP:] = jnp.zeros((NP, NP), BF)
    for k in range(1, GROUP):
        gather[(k - 1) * NP : k * NP] = power_pair(GROUP - 1 - lanes[k])
    for it in range(ITERS):
        for k in range(1, GROUP):
            ahead = lane - lanes[k]
            inside[it, (k - 1) * NP : k * NP] = power_pair(
                jnp.where(ahead > 0, ahead - 1 + it, -1)
            )
        for k in range(1, groups):
            across[it, (k - 1) * NP : k * NP] = power_pair(GROUP * (k - 1) + lane + it)
    ending[...] = exact_dot(first[...], inverse[...])
    loads[4].wait()
    for part in range(6 * NORI):
        lines = pl.ds(part * NP, NP)
        folded = halves(
            jnp.dot(coupling[lines], inverse_pair[:NP], preferred_element_type=F32)
        )
        head, tail = split(folded)
        weights[lines, :NP] = head
        weights[lines, NP:] = tail

    def await_halo(it):
        for d in near:
            @pl.when(has(d))
            def _():
                halo_copy(it, -d).wait_recv()

    await_halo(0)
    own_codes = sent[0, ROWS:]
    gathered = [own_codes if p == DEPTH else halo[0, p, ROWS:] for p in range(SPAN)]
    gathered = [block.astype(F32)[:8] for block in gathered]
    turned = jnp.transpose(
        jnp.concatenate(gathered + [jnp.zeros((NP - 8 * SPAN, NP), F32)], axis=0)
    )
    for place_no in range(SPAN):
        for face in range(6):
            column = place_no * 8 + face
            code = jnp.broadcast_to(turned[:ROWS, column : column + 1], (ROWS, NP)).astype(BF)
            for kind in range(NORI):
                mask[face * NORI + kind, place_no * ROWS : (place_no + 1) * ROWS] = jnp.where(
                    code == jnp.array(kind, BF), jnp.array(1, BF), jnp.array(0, BF)
                )

    steps_here = counts[0]

    def iteration(it, _):
        for place_no in range(SPAN):
            lines = pl.ds(place_no * ROWS, ROWS)
            if place_no == DEPTH:
                current[lines] = state[...]
            else:
                current[lines] = halo[it, place_no, :ROWS].astype(F32)
        now, later = current, following
        for step in range(FSTEPS):
            for sweep in range(SWEEPS):
                reach = FL * (step * SWEEPS + sweep + 1)
                source = now if sweep == 0 else iterate.at[sweep - 1]
                for low, height in row_blocks(reach, EXT - reach):
                    lines = pl.ds(low, height)
                    picked = []
                    for face, shift in enumerate(SHIFTS):
                        rounded = source[pl.ds(low + shift, height)].astype(BF)
                        for kind in range(NORI):
                            picked.append(rounded * mask[face * NORI + kind, lines])
                    coupled = sum(
                        halves(
                            jnp.dot(
                                jnp.concatenate(picked[part : part + 2], axis=1),
                                weights[part * NP : (part + 2) * NP],
                                preferred_element_type=F32,
                            )
                        )
                        for part in range(0, 6 * NORI, 2)
                    )
                    if sweep == 0:
                        ahead = halves(
                            jnp.dot(
                                jnp.concatenate(split(now[lines]), axis=1),
                                inverse_pair[...],
                                preferred_element_type=F32,
                            )
                        )
                        coarse[step, lines] = ahead
                    else:
                        ahead = coarse[step, lines]
                    update = ahead - coupled
                    if sweep < SWEEPS - 1:
                        iterate[sweep, lines] = update
                    else:
                        later[lines] = jnp.where(step < steps_here, update, now[lines])
            now, later = later, now
        own = pl.ds(OWN, ROWS)
        defect = now[own] - coarse[0, own]
        gone[it] = defect.astype(BF)
        for k in range(GROUP - 1, 0, -1):
            defect_copy(it, k).start()
        own_share = halves(
            jnp.dot(
                jnp.concatenate(split(defect), axis=1),
                own_power[...],
                preferred_element_type=F32,
            )
        )
        for k in range(1, GROUP):
            defect_copy(it, k).wait_recv()
        group_defects = jnp.concatenate([come[it, k] for k in range(GROUP - 1)], axis=1)
        sums[it] = (
            own_share + halves(jnp.dot(group_defects, gather[...], preferred_element_type=F32))
        ).astype(BF)
        for k in (2, 3, 1):
            @pl.when(group + k < groups)
            def _():
                sum_copy(it, k).start()
        change = halves(
            jnp.dot(group_defects, inside[it], preferred_element_type=F32)
        )
        for k in (1, 3, 2):
            @pl.when(group >= k)
            def _():
                sum_copy(it, k).wait_recv()
        change += halves(
            jnp.dot(
                jnp.concatenate([older[it, k] for k in range(groups - 1)], axis=1),
                across[it],
                preferred_element_type=F32,
            )
        )

        @pl.when(it == 0)
        def _():
            fresh = first[...] + change
            state[...] = fresh
            sent[1, :ROWS] = fresh.astype(BF)
            for d in offsets:
                @pl.when(has(d))
                def _():
                    halo_copy(1, d).start()
            await_halo(1)

        @pl.when(it == ITERS - 1)
        def _():
            out[...] = ending[...] + defect + change

        return 0

    lax.fori_loop(0, ITERS, iteration, 0)

    for d in offsets:
        @pl.when(has(d))
        def _():
            for it in range(ITERS):
                halo_copy(it, d).wait_send()
    for it in range(ITERS):
        for k in range(1, GROUP):
            defect_copy(it, k).wait_send()
    for k in range(1, groups):
        @pl.when(group + k < groups)
        def _():
            for it in range(ITERS):
                sum_copy(it, k).wait_send()


def solution(mesh):
    tm_size, space_size = mesh.shape["tm"], mesh.shape["space"]
    groups = tm_size // GROUP

    def per_device(initial, inverse, coupling, neighbours, orientation, counts):
        vmem = pl.BlockSpec(memory_space=pltpu.VMEM)
        dma = pltpu.SemaphoreType.DMA

        def body(*refs):
            kernel(tm_size, space_size, *refs)

        finish = pl.pallas_call(
            body,
            out_shape=jax.ShapeDtypeStruct((ROWS, NP), F32),
            in_specs=[pl.BlockSpec(memory_space=pltpu.HBM)] * 5
            + [pl.BlockSpec(memory_space=pltpu.SMEM)],
            out_specs=vmem,
            scratch_shapes=[
                pltpu.VMEM((ROWS, NP), F32),
                pltpu.VMEM((NP, NP), F32),
                pltpu.VMEM((6 * NORI * NP, NP), BF),
                pltpu.VMEM((6, ROWS), jnp.int32),
                pltpu.VMEM((6, ROWS), jnp.int32),
                pltpu.VMEM((tm_size * NP, NP), F32),
                pltpu.VMEM((2 * NP, 2 * NP), BF),
                pltpu.VMEM(((GROUP - 1) * NP, 2 * NP), BF),
                pltpu.VMEM((ITERS, (GROUP - 1) * NP, 2 * NP), BF),
                pltpu.VMEM((ITERS, (groups - 1) * NP, 2 * NP), BF),
                pltpu.VMEM((2 * NP, 2 * NP), BF),
                pltpu.VMEM((6 * NORI * NP, 2 * NP), BF),
                pltpu.VMEM((6 * NORI, EXT, NP), BF),
                pltpu.VMEM((16, NP), F32),
                pltpu.VMEM((ITERS, MESSAGE, NP), BF),
                pltpu.VMEM((ITERS, SPAN, MESSAGE, NP), BF),
                pltpu.VMEM((ITERS, ROWS, NP), BF),
                pltpu.VMEM((ITERS, GROUP - 1, ROWS, NP), BF),
                pltpu.VMEM((ITERS, ROWS, NP), BF),
                pltpu.VMEM((ITERS, groups - 1, ROWS, NP), BF),
                pltpu.VMEM((EXT, NP), F32),
                pltpu.VMEM((EXT, NP), F32),
                pltpu.VMEM((SWEEPS - 1, EXT, NP), F32),
                pltpu.VMEM((FSTEPS, EXT, NP), F32),
                pltpu.VMEM((ROWS, NP), F32),
                pltpu.VMEM((ROWS, NP), F32),
                pltpu.VMEM((ROWS, NP), F32),
                dma((5,)),
                dma((ITERS, SPAN)),
                dma((ITERS, SPAN)),
                dma((ITERS, GROUP - 1)),
                dma((ITERS, GROUP - 1)),
                dma((ITERS, groups - 1)),
                dma((ITERS, groups - 1)),
            ],
            compiler_params=pltpu.CompilerParams(
                collective_id=0, has_side_effects=True, vmem_limit_bytes=40 << 20
            ),
            name="parareal",
        )(
            *(
                pltpu.with_memory_space_constraint(array, pltpu.HBM)
                for array in (
                    initial,
                    inverse,
                    coupling.reshape(6 * NORI * NP, NP),
                    neighbours.T,
                    orientation.T,
                )
            ),
            counts,
        )
        return finish[None]

    return jax.shard_map(
        per_device,
        mesh=mesh,
        in_specs=(P("space", None), P(), P(), P("space", None), P("space", None), P("tm")),
        out_specs=P("tm", "space", None),
        check_vma=False,
    )
```
